32 devices in a mesh: groups: 2 (over x), row: 16 (over z, y, core).
Axes of the slice: x: 2, y: 2, z: 4, core: 2. Of those that a mesh axis runs over, the one named last changes fastest.
Arguments:
- strain: float32 [8192, 3000], P(('groups', 'row')), parts along dimension 0, may hold values from -130 to 130, as said below
- pair_live: int32 [32, 8], P(('groups', 'row')), parts along dimension 0, may hold values 0 or 1
Outputs:
- correlations: bfloat16 [32, 8, 8, 256, 256], P(('groups', 'row')), parts along dimension 0
The draws below stay inside these ranges and needn't reach their ends.
There are 2 independent parts, one for each index of `groups`. The reference program is written for one: setup_inputs(seed, part) draws one part's arguments, and reference() takes and returns one part's arrays. A program takes and returns all parts, laid end to end along the dimension named above; each array names one. Nothing has to cross between parts.
Inputs may be any that keep to these rules, and one draw needn't show every extreme that they name: `strain`: records are a common ground motion seen by all channels with channel-dependent gain, plus each channel's own noise.
All inputs are finite; a program needn't handle non-finite values. No bound on the sum of `pair_live` on one device may be relied on, other than what follows from the above.
Results may differ from the reference program's by a relative error of at most 0.0057.
Values may be sent and summed in bfloat16 or wider, within the bound.
A program may use at most 64 MiB of HBM per device.

```python
import math
import jax
import jax.numpy as jnp
from jax import lax

BLK = 256
NT = 3000
F0 = 60
NF = 512
WB = 64
NLAG = 256
NSRC = 8
BAND = 8
NBLK = 16
CH = 4096
N_ROW = 16


def draw_strain(key, part):
    key = jax.random.fold_in(key, 11)
    key_common, key_noise, key_scale = jax.random.split(key, 3)
    common_mode = jnp.clip(jax.random.normal(key_common, (NT,), jnp.float32), -4.0, 4.0) * 3.0
    position = jnp.arange(CH, dtype=jnp.float32) / (CH - 1)
    channel_gain = 1.0 + 2.0 * position
    noise_value = jnp.clip(jax.random.normal(key_noise, (CH, NT), jnp.float32), -5.0, 5.0)
    noise_scale = jnp.exp(jax.random.uniform(key_scale, (CH, 1), jnp.float32, 0.0, 1.1))
    return channel_gain[:, None] * common_mode[None, :] + noise_value * noise_scale


def place_ends(drawn, own_key, least, high):
    shape = drawn.shape
    spot = [jax.random.randint(jax.random.fold_in(own_key, axis), (), 0, shape[axis]) for axis in range(len(shape))]
    drawn = drawn.at[tuple(spot)].set(least)
    longest = shape.index(max(shape))
    spot[longest] = (spot[longest] + 1) % shape[longest]
    return drawn.at[tuple(spot)].set(high)


def setup_inputs(seed: int = 0, part: int = 0) -> dict:
    splits = jax.random.split(jax.random.key(seed), 3)
    own_keys = jax.random.split(jax.random.fold_in(splits[2], part), 3)
    return {
        "strain": draw_strain(jax.random.fold_in(jax.random.fold_in(splits[2], part), 71), part),
        "pair_live": place_ends((jax.random.randint(own_keys[1], (NBLK, BAND), 0, 4) < 3).astype(jnp.int32), jax.random.fold_in(own_keys[1], 1), 0, 1),
    }


def make_dft():
    t = jnp.arange(NT, dtype=jnp.int32)[:, None]
    f = (F0 + jnp.arange(NF, dtype=jnp.int32))[None, :]
    angles = jnp.mod(t * f, NT).astype(jnp.float32) * (2.0 * math.pi / NT)
    return jnp.concatenate([jnp.cos(angles), -jnp.sin(angles)], axis=1)

def make_lags():
    f = (F0 + jnp.arange(NF, dtype=jnp.int32))[:, None]
    shift_lag = (jnp.arange(NLAG, dtype=jnp.int32) - NLAG // 2)[None, :]
    angles = jnp.mod(f * shift_lag, NT).astype(jnp.float32) * (2.0 * math.pi / NT)
    lag_norm = 1.0 / math.sqrt(NF)
    return (jnp.concatenate([jnp.cos(angles), -jnp.sin(angles)], axis=0) * lag_norm).astype(jnp.bfloat16)

def whiten(spectra, common_mode):
    centred = spectra - common_mode[None, :]
    real_part = centred[:, :NF]
    imag_part = centred[:, NF:]
    power_sum = real_part * real_part + imag_part * imag_part
    band_mean = lax.optimization_barrier(jnp.mean(power_sum.reshape(centred.shape[0], NF // WB, WB), axis=2))
    inv_rms = jnp.repeat(lax.rsqrt(band_mean + 1e-06), WB, axis=1)
    inv_rms = jnp.concatenate([inv_rms, inv_rms], axis=1)
    return (centred * inv_rms).astype(jnp.bfloat16)

def correlate(source_rows, column, lag_basis):
    left = source_rows.astype(jnp.float32)
    right = column.astype(jnp.float32)
    left_re = left[:, None, :NF]
    left_im = left[:, None, NF:]
    right_re = right[None, :, :NF]
    right_im = right[None, :, NF:]
    cross_spec = jnp.concatenate([left_re * right_re + left_im * right_im, left_im * right_re - left_re * right_im], axis=2).astype(jnp.bfloat16)
    product = jnp.dot(cross_spec.reshape(NSRC * BLK, 2 * NF), lag_basis, preferred_element_type=jnp.float32)
    return product.reshape(NSRC, BLK, NLAG).astype(jnp.bfloat16)

def reference(strain, pair_live):
    spectra = jnp.dot(strain, make_dft(), precision=lax.Precision.HIGHEST)
    common_mode = lax.optimization_barrier(jnp.mean(spectra, axis=0))
    whitened = whiten(spectra, common_mode)
    lag_basis = make_lags()
    blocks = whitened.reshape(N_ROW, BLK, 2 * NF)
    sources = blocks.reshape(N_ROW, NSRC, BLK // NSRC, 2 * NF)[:, :, 0, :]

    def one_block(block_index):
        source_rows = lax.dynamic_index_in_dim(sources, block_index, 0, keepdims=False)
        live_row = lax.dynamic_index_in_dim(pair_live, block_index, 0, keepdims=False)
        tile_list = []
        for k in range(BAND):
            target_block = jnp.minimum(block_index + k, N_ROW - 1).astype(jnp.int32)
            column = lax.dynamic_index_in_dim(blocks, target_block, 0, keepdims=False)
            is_live = (live_row[k] > 0) & (block_index + k < N_ROW)
            tile_out = correlate(source_rows, column, lag_basis)
            tile_list.append(jnp.where(is_live, tile_out, jnp.zeros_like(tile_out)))
        return jnp.stack(tile_list)
    return lax.map(one_block, jnp.arange(N_ROW, dtype=jnp.int32))
```

```python
import functools
import math

import jax
import jax.numpy as jnp
import numpy as np
from jax import lax
from jax.experimental import pallas as pl
from jax.experimental.pallas import tpu as pltpu
from jax.sharding import PartitionSpec as P

BLK = 256
NT = 3000
F0 = 60
NF = 512
WB = 64
NLAG = 256
NSRC = 8
BAND = 8

HALF = NT // 2
KPAD = 1536
PLANE = 4
SLOTS = 11
CHUNKS = 4
CROWS = BLK // CHUNKS
HF = NF // 2
MESH = pl.DeviceIdType.MESH
Z, Y, C = 0, 1, 2


def dft_tables():
    out = np.zeros((2, 2, KPAD, NF), jnp.bfloat16)
    t = np.arange(HALF, dtype=np.int64)[:, None]
    for parity in range(2):
        f = (F0 + parity + 2 * np.arange(HF, dtype=np.int64))[None, :]
        angles = np.mod(t * f, NT) * (2.0 * math.pi / NT)
        table = np.concatenate([np.cos(angles), -np.sin(angles)], axis=1).astype(np.float32)
        high = table.astype(jnp.bfloat16)
        out[parity, 0, :HALF] = high
        out[parity, 1, :HALF] = (table - high.astype(np.float32)).astype(jnp.bfloat16)
    return out


def lag_table():
    f = (F0 + np.arange(NF, dtype=np.int64))[:, None]
    lag = (np.arange(NLAG, dtype=np.int64) - NLAG // 2)[None, :]
    angles = np.mod(f * lag, NT) * (2.0 * math.pi / NT)
    re = np.cos(angles) / math.sqrt(NF)
    im = -np.sin(angles) / math.sqrt(NF)
    rows = np.concatenate([re[0::2], im[0::2], re[1::2], im[1::2]], axis=0)
    return rows.astype(np.float32).astype(jnp.bfloat16)


def band_table():
    band = np.arange(HF) // (WB // 2)
    return ((band[:, None] == band[None, :]) / WB).astype(jnp.bfloat16)


def split(value):
    high = value.astype(jnp.bfloat16)
    return high, (value - high.astype(jnp.float32)).astype(jnp.bfloat16)


def dot(left, right):
    return jnp.dot(left, right, preferred_element_type=jnp.float32)


def kernel(
    rows,
    live_ref, strain, table, lags, bands, out,
    x, tab, lagv, bandv, xh, xl, spectra, mine, sums, blk, src, mod, stage,
    load_sem, sum_send, sum_recv, send_sem, recv_sem, out_sem,
):
    me = lax.axis_index("row")
    planes = rows // PLANE
    z = me // PLANE
    p = lax.rem(me, PLANE)

    loads = [
        pltpu.make_async_copy(strain, x, load_sem.at[0]),
        pltpu.make_async_copy(table.at[0, 0], tab.at[0, 0], load_sem.at[1]),
        pltpu.make_async_copy(table.at[0, 1], tab.at[0, 1], load_sem.at[2]),
        pltpu.make_async_copy(table.at[1, 0], tab.at[1, 0], load_sem.at[3]),
        pltpu.make_async_copy(table.at[1, 1], tab.at[1, 1], load_sem.at[4]),
        pltpu.make_async_copy(bands, bandv, load_sem.at[5]),
        pltpu.make_async_copy(lags, lagv, load_sem.at[6]),
    ]
    for load in loads:
        load.start()

    barrier = pltpu.get_barrier_semaphore()

    @pl.loop(1, rows)
    def _(step):
        pl.semaphore_signal(
            barrier, inc=1, device_id={"row": lax.rem(me + step, rows)}, device_id_type=MESH
        )

    loads[0].wait()
    lane = lax.broadcasted_iota(jnp.int32, (CROWS, KPAD), 1)
    for parity in range(2):
        for c in range(CHUNKS):
            rs = slice(c * CROWS, (c + 1) * CROWS)
            first = x[rs, 0:KPAD]
            second = x[rs, HALF:NT]
            second = jnp.concatenate([second, jnp.zeros((CROWS, KPAD - HALF), jnp.float32)], axis=1)
            part = first + second if parity == 0 else first - second
            part = jnp.where(lane < HALF, part, 0.0)
            high, low = split(part)
            xh[rs, :] = high
            xl[rs, :] = low
        loads[1 + 2 * parity].wait()
        loads[2 + 2 * parity].wait()
        spectra[:, parity * NF : (parity + 1) * NF] = (
            dot(xl[...], tab[parity, 0]) + dot(xh[...], tab[parity, 1])
        ) + dot(xh[...], tab[parity, 0])
    mine[0] = jnp.sum(spectra[...], axis=0, keepdims=True)

    pl.semaphore_wait(barrier, rows - 1)

    def sum_copy(slot, other):
        return pltpu.make_async_remote_copy(
            src_ref=mine.at[0],
            dst_ref=sums.at[slot],
            send_sem=sum_send.at[other],
            recv_sem=sum_recv.at[slot],
            device_id={"row": other},
            device_id_type=MESH,
        )

    @pl.loop(1, rows)
    def _(step):
        sum_copy(me, lax.rem(me + step, rows)).start()

    sums[me] = mine[0]
    loads[5].wait()
    loads[6].wait()

    @pl.loop(1, rows)
    def _(step):
        other = lax.rem(me + step, rows)
        sum_copy(other, other).wait_recv()

    common = jnp.sum(sums[...], axis=0) * (1.0 / (rows * BLK))

    def move(kind, slot, c):
        rs = pl.ds(c * CROWS, CROWS)
        target = {
            Z: me - PLANE,
            Y: jnp.where(p < 2, me + 2, me - 2),
            C: jnp.where(lax.rem(p, 2) == 0, me + 1, me - 1),
        }[kind]
        to = slot + PLANE if kind == Z else slot
        return pltpu.make_async_remote_copy(
            src_ref=blk.at[slot, rs],
            dst_ref=blk.at[to, rs],
            send_sem=send_sem.at[kind, slot, c],
            recv_sem=recv_sem.at[to, c],
            device_id={"row": target},
            device_id_type=MESH,
        )

    sent = []

    def send(when, kind, slot, c):
        sent.append((when, kind, slot, c))

        @pl.when(when)
        def _():
            move(kind, slot, c).start()

    def arrive(when, slot, c):
        @pl.when(when)
        def _():
            pltpu.make_async_copy(
                blk.at[slot, pl.ds(c * CROWS, CROWS)],
                blk.at[slot, pl.ds(c * CROWS, CROWS)],
                recv_sem.at[slot, c],
            ).wait()

    low_plane = z > 0
    has_b = z < planes - 1
    has_c = z < planes - 2
    left = p < 2

    for c in range(CHUNKS):
        rs = slice(c * CROWS, (c + 1) * CROWS)
        centred = spectra[rs, :] - common
        parts = [centred[:, q * HF : (q + 1) * HF] for q in range(4)]
        power = (parts[0] * parts[0] + parts[1] * parts[1]) + (
            parts[2] * parts[2] + parts[3] * parts[3]
        )
        high, low = split(power)
        mean = dot(high, bandv[...]) + dot(low, bandv[...])
        scale = lax.rsqrt(mean + 1e-06)
        white = jnp.concatenate([part * scale for part in parts], axis=1).astype(jnp.bfloat16)
        blk[p, rs, :] = white
        wide = white.astype(jnp.float32)
        src[2 * c : 2 * c + 1, :] = wide[0:1]
        src[2 * c + 1 : 2 * c + 2, :] = wide[32:33]
        send(low_plane, Z, p, c)
        send(jnp.logical_not(left), Y, p, c)
        send(lax.rem(p, 2) == 1, C, p, c)

    columns = jnp.transpose(src[...])
    for s in range(NSRC):
        for parity in range(2):
            r0, i0, e0 = parity * NF, parity * NF + HF, parity * NF + NF
            ar = columns[r0:i0, s : s + 1]
            ai = columns[i0:e0, s : s + 1]
            lr = lagv[r0:i0, :].astype(jnp.float32)
            li = lagv[i0:e0, :].astype(jnp.float32)
            mod[s, r0:i0, :] = (ar * lr + ai * li).astype(jnp.bfloat16)
            mod[s, i0:e0, :] = (ai * lr - ar * li).astype(jnp.bfloat16)

    def correlate(k):
        if k >= 2:
            flush(k - 2).wait()
        is_live = (live_ref[0, k] > 0) & (me + k < rows)

        @pl.loop(0, NSRC)
        def _(s):
            product = dot(blk[p + k], mod[s])
            stage[k % 2, s] = jnp.where(is_live, product, 0.0).astype(jnp.bfloat16)

        flush(k).start()

    def flush(k):
        return pltpu.make_async_copy(stage.at[k % 2], out.at[0, k], out_sem.at[k % 2])

    def a_across(c):
        arrive(left, p + 2, c)
        send(left, C, p + 2, c)

    def b_down(c):
        arrive(has_b, p + 4, c)
        send(has_b & low_plane & (p < 3), Z, p + 4, c)
        send(has_b, Y, p + 4, c)
        send(has_b, C, p + 4, c)

    def b_across(c, when):
        slot = 4 + lax.rem(p + 2, 4)
        arrive(has_b & when, slot, c)
        send(has_b & when, C, slot, c)

    def c_down(c):
        slot = jnp.minimum(p, 2) + 8
        arrive(has_c & (p < 3), slot, c)
        send(has_c & left, Y, slot, c)
        send(has_c & ((p == 0) | (p == 2)), C, slot, c)

    def c_across(c):
        slot = jnp.maximum(p, 2) + 6
        arrive(has_c & jnp.logical_not(left), slot, c)
        send(has_c & jnp.logical_not(left), C, slot, c)

    def final(k):
        slot = p + k
        beside_a = (slot < 4) & ((k == 1) & (lax.rem(p, 2) == 0) | left & (k != 2) & (slot > 1))
        beside_b = has_b & (slot >= 4) & (slot < 8) & (lax.rem(slot, 2) != lax.rem(p, 2))
        beside_c = has_c & (slot >= 8) & (
            (p == 1) | (p == 2) & (slot == 9) | (p == 3) & (slot != 9)
        )
        for c in range(CHUNKS):
            arrive(beside_a | beside_b | beside_c, slot, c)

    right = jnp.logical_not(left)
    correlate(0)
    for c in range(CHUNKS):
        a_across(c)
        b_down(c)
        if c > 0:
            b_across(c - 1, right)
    b_across(CHUNKS - 1, right)
    for k in range(1, 4):
        final(k)
        correlate(k)
        c_down(k - 1)
        b_across(k - 1, left)
        c_across(k - 1)
    c_down(CHUNKS - 1)
    b_across(CHUNKS - 1, left)
    c_across(CHUNKS - 1)
    for k in range(4, BAND):
        final(k)
        correlate(k)

    for when, kind, slot, c in sent:

        @pl.when(when)
        def _(kind=kind, slot=slot, c=c):
            move(kind, slot, c).wait_send()

    @pl.loop(1, rows)
    def _(step):
        other = lax.rem(me + step, rows)
        sum_copy(me, other).wait_send()

    flush(BAND - 2).wait()
    flush(BAND - 1).wait()


def on_device(rows, strain, pair_live):
    anywhere = pl.BlockSpec(memory_space=pl.ANY)
    f32, b16 = jnp.float32, jnp.bfloat16
    dma = pltpu.SemaphoreType.DMA
    return pl.pallas_call(
        functools.partial(kernel, rows),
        out_shape=jax.ShapeDtypeStruct((1, BAND, NSRC, BLK, NLAG), b16),
        in_specs=[pl.BlockSpec(memory_space=pltpu.SMEM)] + [anywhere] * 4,
        out_specs=anywhere,
        scratch_shapes=[
            pltpu.VMEM((BLK, NT), f32),
            pltpu.VMEM((2, 2, KPAD, NF), b16),
            pltpu.VMEM((2 * NF, NLAG), b16),
            pltpu.VMEM((HF, HF), b16),
            pltpu.VMEM((BLK, KPAD), b16),
            pltpu.VMEM((BLK, KPAD), b16),
            pltpu.VMEM((BLK, 2 * NF), f32),
            pltpu.VMEM((1, 1, 2 * NF), f32),
            pltpu.VMEM((rows, 1, 2 * NF), f32),
            pltpu.VMEM((SLOTS, BLK, 2 * NF), b16),
            pltpu.VMEM((NSRC, 2 * NF), f32),
            pltpu.VMEM((NSRC, 2 * NF, NLAG), b16),
            pltpu.VMEM((2, NSRC, BLK, NLAG), b16),
            dma((7,)),
            dma((rows,)),
            dma((rows,)),
            dma((3, SLOTS, CHUNKS)),
            dma((SLOTS, CHUNKS)),
            dma((2,)),
        ],
        compiler_params=pltpu.CompilerParams(
            collective_id=0, has_side_effects=True, vmem_limit_bytes=56 * 1024 * 1024
        ),
        cost_estimate=pl.CostEstimate(
            flops=12_000_000_000, bytes_accessed=20_000_000, transcendentals=0
        ),
    )(pair_live, strain, jnp.asarray(dft_tables()), jnp.asarray(lag_table()), jnp.asarray(band_table()))


def solution(mesh):
    rows = mesh.shape["row"]
    return jax.shard_map(
        functools.partial(on_device, rows),
        mesh=mesh,
        in_specs=(P(("groups", "row"), None), P(("groups", "row"), None)),
        out_specs=P(("groups", "row"), None, None, None, None),
        check_vma=False,
    )
```

```python
import functools
import math

import jax
import jax.numpy as jnp
import numpy as np
from jax import lax
from jax.experimental import pallas as pl
from jax.experimental.pallas import tpu as pltpu
from jax.sharding import PartitionSpec as P

BLK = 256
NT = 3000
F0 = 60
NF = 512
WB = 64
NLAG = 256
NSRC = 8
BAND = 8

HALF = NT // 2
KPAD = 1536
PLANE = 4
SLOTS = 11
CHUNKS = 4
CROWS = BLK // CHUNKS
HF = NF // 2
MESH = pl.DeviceIdType.MESH
Z, Y, C = 0, 1, 2


def dft_tables():
    out = np.zeros((2, 2, NF, KPAD), jnp.bfloat16)
    t = np.arange(HALF, dtype=np.int64)[None, :]
    for parity in range(2):
        f = (F0 + parity + 2 * np.arange(HF, dtype=np.int64))[:, None]
        angles = np.mod(t * f, NT) * (2.0 * math.pi / NT)
        table = np.concatenate([np.cos(angles), -np.sin(angles)], axis=0).astype(np.float32)
        high = table.astype(jnp.bfloat16)
        out[parity, 0, :, :HALF] = high
        out[parity, 1, :, :HALF] = (table - high.astype(np.float32)).astype(jnp.bfloat16)
    return out


def lag_table():
    f = (F0 + np.arange(NF, dtype=np.int64))[:, None]
    lag = (np.arange(NLAG, dtype=np.int64) - NLAG // 2)[None, :]
    angles = np.mod(f * lag, NT) * (2.0 * math.pi / NT)
    re = np.cos(angles) / math.sqrt(NF)
    im = -np.sin(angles) / math.sqrt(NF)
    rows = np.concatenate([re[0::2], im[0::2], re[1::2], im[1::2]], axis=0)
    return rows.astype(np.float32).astype(jnp.bfloat16)


def band_table():
    band = np.arange(HF) // (WB // 2)
    return ((band[:, None] == band[None, :]) / WB).astype(jnp.bfloat16)


def split(value):
    high = value.astype(jnp.bfloat16)
    return high, (value - high.astype(jnp.float32)).astype(jnp.bfloat16)


def dot(left, right):
    return jnp.dot(left, right, preferred_element_type=jnp.float32)


def in_row(tile):
    return jnp.concatenate([tile[q : q + 1, :] for q in range(8)], axis=1)


def kernel(
    rows,
    live_ref, strain, table, lags, bands, out,
    x, tab, lagv, bandv, xh, xl, spectra, mine, sums, blk, wh, src, mod,
    load_sem, sum_send, sum_recv, send_sem, recv_sem,
):
    me = lax.axis_index("row")
    planes = rows // PLANE
    z = me // PLANE
    p = lax.rem(me, PLANE)

    loads = [
        pltpu.make_async_copy(strain, x, load_sem.at[0]),
        pltpu.make_async_copy(table.at[0, 0], tab.at[0, 0], load_sem.at[1]),
        pltpu.make_async_copy(table.at[0, 1], tab.at[0, 1], load_sem.at[2]),
        pltpu.make_async_copy(table.at[1, 0], tab.at[1, 0], load_sem.at[3]),
        pltpu.make_async_copy(table.at[1, 1], tab.at[1, 1], load_sem.at[4]),
        pltpu.make_async_copy(bands, bandv, load_sem.at[5]),
        pltpu.make_async_copy(lags, lagv, load_sem.at[6]),
    ]
    for load in loads:
        load.start()

    barrier = pltpu.get_barrier_semaphore()

    @pl.loop(1, rows)
    def _(step):
        pl.semaphore_signal(
            barrier, inc=1, device_id={"row": lax.rem(me + step, rows)}, device_id_type=MESH
        )

    loads[0].wait()
    for r0 in range(0, KPAD, CROWS):
        count = min(CROWS, HALF - r0)
        rs = slice(r0, r0 + CROWS)
        for parity in range(2):
            first = x[r0 : r0 + count, :]
            second = x[HALF + r0 : HALF + r0 + count, :]
            part = first + second if parity == 0 else first - second
            if count < CROWS:
                part = jnp.concatenate([part, jnp.zeros((CROWS - count, BLK), jnp.float32)], axis=0)
            high, low = split(part)
            xh[parity, rs, :] = high
            xl[parity, rs, :] = low
    for parity in range(2):
        loads[1 + 2 * parity].wait()
        loads[2 + 2 * parity].wait()
        turned = (
            dot(tab[parity, 0], xl[parity]) + dot(tab[parity, 1], xh[parity])
        ) + dot(tab[parity, 0], xh[parity])
        spectra[:, parity * NF : (parity + 1) * NF] = jnp.transpose(turned)
    block_sum = jnp.sum(spectra[...], axis=0, keepdims=True)
    for q in range(8):
        mine[0, q : q + 1, :] = block_sum[:, q * 128 : (q + 1) * 128]

    own_mean = block_sum * (1.0 / BLK)
    blk[p] = (spectra[...] - own_mean).astype(jnp.bfloat16)

    pl.semaphore_wait(barrier, rows - 1)

    def sum_copy(slot, other):
        return pltpu.make_async_remote_copy(
            src_ref=mine.at[0],
            dst_ref=sums.at[slot],
            send_sem=sum_send.at[other],
            recv_sem=sum_recv.at[slot],
            device_id={"row": other},
            device_id_type=MESH,
        )

    @pl.loop(1, rows)
    def _(step):
        sum_copy(me, lax.rem(me + step, rows)).start()

    sums[me] = mine[0]

    def move(kind, slot, c):
        rs = pl.ds(c * CROWS, CROWS)
        target = {
            Z: me - PLANE,
            Y: jnp.where(p < 2, me + 2, me - 2),
            C: jnp.where(lax.rem(p, 2) == 0, me + 1, me - 1),
        }[kind]
        to = slot + PLANE if kind == Z else slot
        return pltpu.make_async_remote_copy(
            src_ref=blk.at[slot, rs],
            dst_ref=blk.at[to, rs],
            send_sem=send_sem.at[kind, slot, c],
            recv_sem=recv_sem.at[to, c],
            device_id={"row": target},
            device_id_type=MESH,
        )

    sent = []

    def send(when, kind, slot, c):
        sent.append((when, kind, slot, c))

        @pl.when(when)
        def _():
            move(kind, slot, c).start()

    def arrive(when, slot, c):
        @pl.when(when)
        def _():
            pltpu.make_async_copy(
                blk.at[slot, pl.ds(c * CROWS, CROWS)],
                blk.at[slot, pl.ds(c * CROWS, CROWS)],
                recv_sem.at[slot, c],
            ).wait()

    low_plane = z > 0
    has_b = z < planes - 1
    has_c = z < planes - 2
    left = p < 2

    for c in range(CHUNKS):
        send(low_plane, Z, p, c)
        send(jnp.logical_not(left), Y, p, c)
        send(lax.rem(p, 2) == 1, C, p, c)

    def common_mode():
        @pl.loop(1, rows)
        def _(step):
            other = lax.rem(me + step, rows)
            sum_copy(other, other).wait_recv()

        return in_row(jnp.sum(sums[...], axis=0)) * (1.0 / (rows * BLK))

    def whiten(centred):
        parts = [centred[:, q * HF : (q + 1) * HF] for q in range(4)]
        power = (parts[0] * parts[0] + parts[1] * parts[1]) + (
            parts[2] * parts[2] + parts[3] * parts[3]
        )
        high, low = split(power)
        mean = dot(high, bandv[...]) + dot(low, bandv[...])
        scale = lax.rsqrt(mean + 1e-06)
        return jnp.concatenate([part * scale for part in parts], axis=1).astype(jnp.bfloat16)

    def prepare(common):
        for c in range(CHUNKS):
            rs = slice(c * CROWS, (c + 1) * CROWS)
            white = whiten(spectra[rs, :] - common)
            wh[0, rs, :] = white
            wide = white.astype(jnp.float32)
            src[2 * c : 2 * c + 1, :] = wide[0:1]
            src[2 * c + 1 : 2 * c + 2, :] = wide[32:33]

        columns = jnp.transpose(src[...])
        for s in range(NSRC):
            for parity in range(2):
                r0, i0, e0 = parity * NF, parity * NF + HF, parity * NF + NF
                ar = columns[r0:i0, s : s + 1]
                ai = columns[i0:e0, s : s + 1]
                lr = lagv[r0:i0, :].astype(jnp.float32)
                li = lagv[i0:e0, :].astype(jnp.float32)
                mod[s, r0:i0, :] = (ar * lr + ai * li).astype(jnp.bfloat16)
                mod[s, i0:e0, :] = (ai * lr - ar * li).astype(jnp.bfloat16)

    def correlate(k, common):
        is_live = (live_ref[0, k] > 0) & (me + k < rows)

        if k > 0:
            shift = in_row(sums[jnp.minimum(me + k, rows - 1)]) * (1.0 / BLK) - common

            @pl.loop(0, CHUNKS)
            def _(c):
                rs = pl.ds(pl.multiple_of(c * CROWS, CROWS), CROWS)
                wh[k % 2, rs, :] = whiten(blk[p + k, rs, :].astype(jnp.float32) + shift)

        @pl.loop(0, NSRC, unroll=8)
        def _(s):
            product = dot(wh[k % 2], mod[s])
            out[0, k, s] = jnp.where(is_live, product, 0.0).astype(jnp.bfloat16)

    def a_across(c):
        arrive(left, p + 2, c)
        send(left, C, p + 2, c)

    def b_down(c):
        arrive(has_b, p + 4, c)
        send(has_b & low_plane & ((p == 0) | (p == 2)), Z, p + 4, c)
        send(has_b, Y, p + 4, c)
        send(has_b, C, p + 4, c)

    def b_across(c, when):
        slot = 4 + lax.rem(p + 2, 4)
        arrive(has_b & when, slot, c)
        send(has_b & when, C, slot, c)
        send(has_b & low_plane & (p == 3) & when, Z, slot, c)

    def c_down(c):
        slot = jnp.where(p == 3, 1, jnp.minimum(p, 2)) + 8
        arrive(has_c & (p != 1), slot, c)
        send(has_c & (p == 0), Y, slot, c)
        send(has_c & (p != 1), C, slot, c)

    def c_across(c):
        arrive(has_c & (p == 2), 8, c)
        send(has_c & (p == 2), C, 8, c)

    def final(k):
        slot = p + k
        beside_a = (slot < 4) & ((k == 1) & (lax.rem(p, 2) == 0) | left & (k != 2) & (slot > 1))
        beside_b = has_b & (slot >= 4) & (slot < 8) & (lax.rem(slot, 2) != lax.rem(p, 2))
        beside_c = has_c & (slot >= 8) & (
            (p == 1) | (p == 2) & (slot == 9) | (p == 3) & (slot != 9)
        )
        for c in range(CHUNKS):
            arrive(beside_a | beside_b | beside_c, slot, c)

    right = jnp.logical_not(left)

    def first(c):
        a_across(c)
        b_down(c)
        if c > 0:
            b_across(c - 1, right)

    def second(c):
        c_down(c)
        b_across(c, left)
        c_across(c)

    def pair(k):
        final(k)
        correlate(k, common)

    first(0)
    loads[5].wait()
    loads[6].wait()
    common = common_mode()
    prepare(common)
    first(1)
    correlate(0, common)
    first(2)
    first(3)
    b_across(CHUNKS - 1, right)
    pair(1)
    second(0)
    pair(2)
    second(1)
    pair(3)
    second(2)
    pair(4)
    second(3)
    pair(5)
    pair(6)
    pair(7)

    for when, kind, slot, c in sent:

        @pl.when(when)
        def _(kind=kind, slot=slot, c=c):
            move(kind, slot, c).wait_send()

    @pl.loop(1, rows)
    def _(step):
        other = lax.rem(me + step, rows)
        sum_copy(me, other).wait_send()


def write_out(result, out, sem):
    copies = [pltpu.make_async_copy(result.at[0, k], out.at[0, k], sem.at[k]) for k in range(BAND)]
    for copy in copies:
        copy.start()
    for copy in copies:
        copy.wait()


def on_device(rows, strain, pair_live):
    anywhere = pl.BlockSpec(memory_space=pltpu.HBM)
    local = pl.BlockSpec(memory_space=pltpu.VMEM)
    f32, b16 = jnp.float32, jnp.bfloat16
    dma = pltpu.SemaphoreType.DMA
    shape = (1, BAND, NSRC, BLK, NLAG)
    result = pl.pallas_call(
        functools.partial(kernel, rows),
        out_shape=pltpu.VMEM(shape, b16),
        in_specs=[pl.BlockSpec(memory_space=pltpu.SMEM)] + [anywhere] * 4,
        out_specs=local,
        scratch_shapes=[
            pltpu.VMEM((NT, BLK), f32),
            pltpu.VMEM((2, 2, NF, KPAD), b16),
            pltpu.VMEM((2 * NF, NLAG), b16),
            pltpu.VMEM((HF, HF), b16),
            pltpu.VMEM((2, KPAD, BLK), b16),
            pltpu.VMEM((2, KPAD, BLK), b16),
            pltpu.VMEM((BLK, 2 * NF), f32),
            pltpu.VMEM((1, 8, NF // 4), f32),
            pltpu.VMEM((rows, 8, NF // 4), f32),
            pltpu.VMEM((SLOTS, BLK, 2 * NF), b16),
            pltpu.VMEM((2, BLK, 2 * NF), b16),
            pltpu.VMEM((NSRC, 2 * NF), f32),
            pltpu.VMEM((NSRC, 2 * NF, NLAG), b16),
            dma((7,)),
            dma((rows,)),
            dma((rows,)),
            dma((3, SLOTS, CHUNKS)),
            dma((SLOTS, CHUNKS)),
        ],
        compiler_params=pltpu.CompilerParams(
            collective_id=0, has_side_effects=True, vmem_limit_bytes=53 * 1024 * 1024
        ),
        cost_estimate=pl.CostEstimate(
            flops=12_000_000_000, bytes_accessed=20_000_000, transcendentals=0
        ),
    )(pair_live, strain.T, jnp.asarray(dft_tables()), jnp.asarray(lag_table()), jnp.asarray(band_table()))
    return pl.pallas_call(
        write_out,
        out_shape=jax.ShapeDtypeStruct(shape, b16),
        in_specs=[local],
        out_specs=anywhere,
        scratch_shapes=[dma((BAND,))],
        compiler_params=pltpu.CompilerParams(vmem_limit_bytes=12 * 1024 * 1024),
        cost_estimate=pl.CostEstimate(flops=0, bytes_accessed=8_400_000, transcendentals=0),
    )(result)


def solution(mesh):
    rows = mesh.shape["row"]
    return jax.shard_map(
        functools.partial(on_device, rows),
        mesh=mesh,
        in_specs=(P(("groups", "row"), None), P(("groups", "row"), None)),
        out_specs=P(("groups", "row"), None, None, None, None),
        check_vma=False,
    )
```

```python
import functools
import math

import jax
import jax.numpy as jnp
import numpy as np
from jax import lax
from jax.experimental import pallas as pl
from jax.experimental.pallas import tpu as pltpu
from jax.sharding import PartitionSpec as P

BLK = 256
NT = 3000
F0 = 60
NF = 512
WB = 64
NLAG = 256
NSRC = 8
BAND = 8

HALF = NT // 2
KPAD = 1536
DONE = BAND - 2
PLANE = 4
SLOTS = 11
CHUNKS = 4
CROWS = BLK // CHUNKS
HF = NF // 2
MESH = pl.DeviceIdType.MESH
Z, Y, C = 0, 1, 2


def dft_tables():
    out = np.zeros((2, NF, KPAD), jnp.bfloat16)
    t = np.arange(HALF, dtype=np.int64)[None, :]
    for parity in range(2):
        f = (F0 + parity + 2 * np.arange(HF, dtype=np.int64))[:, None]
        angles = np.mod(t * f, NT) * (2.0 * math.pi / NT)
        table = np.concatenate([np.cos(angles), -np.sin(angles)], axis=0).astype(np.float32)
        out[parity, :, :HALF] = table.astype(jnp.bfloat16)
    return out


def lag_table():
    f = (F0 + np.arange(NF, dtype=np.int64))[:, None]
    lag = (np.arange(NLAG, dtype=np.int64) - NLAG // 2)[None, :]
    angles = np.mod(f * lag, NT) * (2.0 * math.pi / NT)
    re = np.cos(angles) / math.sqrt(NF)
    im = -np.sin(angles) / math.sqrt(NF)
    rows = np.concatenate([re[0::2], im[0::2], re[1::2], im[1::2]], axis=0)
    return rows.astype(np.float32).astype(jnp.bfloat16)


def band_table():
    band = np.arange(HF) // (WB // 2)
    return ((band[:, None] == band[None, :]) / WB).astype(jnp.bfloat16)


def split(value):
    high = value.astype(jnp.bfloat16)
    return high, (value - high.astype(jnp.float32)).astype(jnp.bfloat16)


def dot(left, right):
    return jnp.dot(left, right, preferred_element_type=jnp.float32)


def in_row(tile):
    return jnp.concatenate([tile[q : q + 1, :] for q in range(8)], axis=1)


def kernel(
    rows,
    live_ref, strain, table, lags, bands, out, wh, mod,
    x, tab, lagv, bandv, xh, xl, spectra, mine, sums, blk, src,
    load_sem, sum_send, sum_recv, send_sem, recv_sem,
):
    me = lax.axis_index("row")
    planes = rows // PLANE
    z = me // PLANE
    p = lax.rem(me, PLANE)

    loads = [
        pltpu.make_async_copy(strain, x, load_sem.at[0]),
        pltpu.make_async_copy(table.at[0], tab.at[0], load_sem.at[1]),
        pltpu.make_async_copy(table.at[1], tab.at[1], load_sem.at[2]),
        pltpu.make_async_copy(bands, bandv, load_sem.at[3]),
        pltpu.make_async_copy(lags, lagv, load_sem.at[4]),
    ]
    for load in loads:
        load.start()

    barrier = pltpu.get_barrier_semaphore()

    @pl.loop(1, rows)
    def _(step):
        pl.semaphore_signal(
            barrier, inc=1, device_id={"row": lax.rem(me + step, rows)}, device_id_type=MESH
        )

    loads[0].wait()
    for r0 in range(0, KPAD, CROWS):
        count = min(CROWS, HALF - r0)
        rs = slice(r0, r0 + CROWS)
        for parity in range(2):
            first = x[r0 : r0 + count, :]
            second = x[HALF + r0 : HALF + r0 + count, :]
            part = first + second if parity == 0 else first - second
            if count < CROWS:
                part = jnp.concatenate([part, jnp.zeros((CROWS - count, BLK), jnp.float32)], axis=0)
            high, low = split(part)
            xh[parity, rs, :] = high
            xl[parity, rs, :] = low
    for parity in range(2):
        loads[1 + parity].wait()
        turned = dot(tab[parity], xl[parity]) + dot(tab[parity], xh[parity])
        spectra[:, parity * NF : (parity + 1) * NF] = jnp.transpose(turned)
    block_sum = jnp.sum(spectra[...], axis=0, keepdims=True)
    for q in range(8):
        mine[0, q : q + 1, :] = block_sum[:, q * 128 : (q + 1) * 128]

    own_mean = block_sum * (1.0 / BLK)
    blk[p] = (spectra[...] - own_mean).astype(jnp.bfloat16)

    pl.semaphore_wait(barrier, rows - 1)

    def sum_copy(slot, other):
        return pltpu.make_async_remote_copy(
            src_ref=mine.at[0],
            dst_ref=sums.at[slot],
            send_sem=sum_send.at[other],
            recv_sem=sum_recv.at[slot],
            device_id={"row": other},
            device_id_type=MESH,
        )

    @pl.loop(1, rows)
    def _(step):
        sum_copy(me, lax.rem(me + step, rows)).start()

    sums[me] = mine[0]

    def move(kind, slot, c):
        rs = pl.ds(c * CROWS, CROWS)
        target = {
            Z: me - PLANE,
            Y: jnp.where(p < 2, me + 2, me - 2),
            C: jnp.where(lax.rem(p, 2) == 0, me + 1, me - 1),
        }[kind]
        to = slot + PLANE if kind == Z else slot
        return pltpu.make_async_remote_copy(
            src_ref=blk.at[slot, rs],
            dst_ref=blk.at[to, rs],
            send_sem=send_sem.at[kind, slot, c],
            recv_sem=recv_sem.at[to, c],
            device_id={"row": target},
            device_id_type=MESH,
        )

    sent = []

    def send(when, kind, slot, c):
        sent.append((when, kind, slot, c))

        @pl.when(when)
        def _():
            move(kind, slot, c).start()

    def arrive(when, slot, c):
        @pl.when(when)
        def _():
            pltpu.make_async_copy(
                blk.at[slot, pl.ds(c * CROWS, CROWS)],
                blk.at[slot, pl.ds(c * CROWS, CROWS)],
                recv_sem.at[slot, c],
            ).wait()

    low_plane = z > 0
    has_b = z < planes - 1
    has_c = z < planes - 2
    left = p < 2

    for c in range(CHUNKS):
        send(low_plane, Z, p, c)
        send(jnp.logical_not(left), Y, p, c)
        send(lax.rem(p, 2) == 1, C, p, c)

    def common_mode():
        @pl.loop(1, rows)
        def _(step):
            other = lax.rem(me + step, rows)
            sum_copy(other, other).wait_recv()

        return in_row(jnp.sum(sums[...], axis=0)) * (1.0 / (rows * BLK))

    def whiten(centred):
        parts = [centred[:, q * HF : (q + 1) * HF] for q in range(4)]
        power = (parts[0] * parts[0] + parts[1] * parts[1]) + (
            parts[2] * parts[2] + parts[3] * parts[3]
        )
        high, low = split(power)
        mean = dot(high, bandv[...]) + dot(low, bandv[...])
        scale = lax.rsqrt(mean + 1e-06)
        return jnp.concatenate([part * scale for part in parts], axis=1).astype(jnp.bfloat16)

    def prepare(common):
        for c in range(CHUNKS):
            rs = slice(c * CROWS, (c + 1) * CROWS)
            white = whiten(spectra[rs, :] - common)
            wh[0, rs, :] = white
            wide = white.astype(jnp.float32)
            src[2 * c : 2 * c + 1, :] = wide[0:1]
            src[2 * c + 1 : 2 * c + 2, :] = wide[32:33]

        columns = jnp.transpose(src[...])
        for s in range(NSRC):
            for parity in range(2):
                r0, i0, e0 = parity * NF, parity * NF + HF, parity * NF + NF
                ar = columns[r0:i0, s : s + 1]
                ai = columns[i0:e0, s : s + 1]
                lr = lagv[r0:i0, :].astype(jnp.float32)
                li = lagv[i0:e0, :].astype(jnp.float32)
                mod[s, r0:i0, :] = (ar * lr + ai * li).astype(jnp.bfloat16)
                mod[s, i0:e0, :] = (ai * lr - ar * li).astype(jnp.bfloat16)

    def correlate(k, common):
        is_live = (live_ref[0, k] > 0) & (me + k < rows)

        if k > 0:
            shift = in_row(sums[jnp.minimum(me + k, rows - 1)]) * (1.0 / BLK) - common

            @pl.loop(0, CHUNKS)
            def _(c):
                rs = pl.ds(pl.multiple_of(c * CROWS, CROWS), CROWS)
                white = whiten(blk[p + k, rs, :].astype(jnp.float32) + shift)
                if k >= DONE:
                    white = jnp.where(is_live, white, 0.0).astype(jnp.bfloat16)
                wh[k % 2, rs, :] = white

        if k >= DONE:
            return

        @pl.loop(0, NSRC, unroll=8)
        def _(s):
            product = dot(wh[k % 2], mod[s])
            out[k, s] = jnp.where(is_live, product, 0.0).astype(jnp.bfloat16)

    def a_across(c):
        arrive(left, p + 2, c)
        send(left, C, p + 2, c)

    def b_down(c):
        arrive(has_b, p + 4, c)
        send(has_b & low_plane & ((p == 0) | (p == 2)), Z, p + 4, c)
        send(has_b, Y, p + 4, c)
        send(has_b, C, p + 4, c)

    def b_across(c, when):
        slot = 4 + lax.rem(p + 2, 4)
        arrive(has_b & when, slot, c)
        send(has_b & when, C, slot, c)
        send(has_b & low_plane & (p == 3) & when, Z, slot, c)

    def c_down(c):
        slot = jnp.where(p == 3, 1, jnp.minimum(p, 2)) + 8
        arrive(has_c & (p != 1), slot, c)
        send(has_c & (p == 0), Y, slot, c)
        send(has_c & (p != 1), C, slot, c)

    def c_across(c):
        arrive(has_c & (p == 2), 8, c)
        send(has_c & (p == 2), C, 8, c)

    def final(k):
        slot = p + k
        beside_a = (slot < 4) & ((k == 1) & (lax.rem(p, 2) == 0) | left & (k != 2) & (slot > 1))
        beside_b = has_b & (slot >= 4) & (slot < 8) & (lax.rem(slot, 2) != lax.rem(p, 2))
        beside_c = has_c & (slot >= 8) & (
            (p == 1) | (p == 2) & (slot == 9) | (p == 3) & (slot != 9)
        )
        for c in range(CHUNKS):
            arrive(beside_a | beside_b | beside_c, slot, c)

    right = jnp.logical_not(left)

    def first(c):
        a_across(c)
        b_down(c)
        if c > 0:
            b_across(c - 1, right)

    def second(c):
        c_down(c)
        b_across(c, left)
        c_across(c)

    def pair(k):
        final(k)
        correlate(k, common)

    first(0)
    loads[3].wait()
    loads[4].wait()
    common = common_mode()
    prepare(common)
    first(1)
    correlate(0, common)
    first(2)
    first(3)
    b_across(CHUNKS - 1, right)
    pair(1)
    second(0)
    pair(2)
    second(1)
    pair(3)
    second(2)
    pair(4)
    second(3)
    pair(5)
    pair(6)
    pair(7)

    for when, kind, slot, c in sent:

        @pl.when(when)
        def _(kind=kind, slot=slot, c=c):
            move(kind, slot, c).wait_send()

    @pl.loop(1, rows)
    def _(step):
        other = lax.rem(me + step, rows)
        sum_copy(me, other).wait_send()


def write_out(result, wh, mod, out, stage, sem, late_sem):
    copies = [pltpu.make_async_copy(result.at[k], out.at[0, k], sem.at[k]) for k in range(DONE)]
    for copy in copies:
        copy.start()
    for k in range(DONE, BAND):
        for s in range(NSRC):
            stage[k - DONE, s] = dot(wh[k % 2], mod[s]).astype(jnp.bfloat16)
            copies.append(
                pltpu.make_async_copy(
                    stage.at[k - DONE, s], out.at[0, k, s], late_sem.at[k - DONE, s]
                )
            )
            copies[-1].start()
    for copy in copies:
        copy.wait()


def on_device(rows, strain, pair_live):
    anywhere = pl.BlockSpec(memory_space=pltpu.HBM)
    local = pl.BlockSpec(memory_space=pltpu.VMEM)
    f32, b16 = jnp.float32, jnp.bfloat16
    dma = pltpu.SemaphoreType.DMA
    shape = (1, BAND, NSRC, BLK, NLAG)
    results = pl.pallas_call(
        functools.partial(kernel, rows),
        out_shape=[
            pltpu.VMEM((DONE, NSRC, BLK, NLAG), b16),
            pltpu.VMEM((2, BLK, 2 * NF), b16),
            pltpu.VMEM((NSRC, 2 * NF, NLAG), b16),
        ],
        in_specs=[pl.BlockSpec(memory_space=pltpu.SMEM)] + [anywhere] * 4,
        out_specs=[local] * 3,
        scratch_shapes=[
            pltpu.VMEM((NT, BLK), f32),
            pltpu.VMEM((2, NF, KPAD), b16),
            pltpu.VMEM((2 * NF, NLAG), b16),
            pltpu.VMEM((HF, HF), b16),
            pltpu.VMEM((2, KPAD, BLK), b16),
            pltpu.VMEM((2, KPAD, BLK), b16),
            pltpu.VMEM((BLK, 2 * NF), f32),
            pltpu.VMEM((1, 8, NF // 4), f32),
            pltpu.VMEM((rows, 8, NF // 4), f32),
            pltpu.VMEM((SLOTS, BLK, 2 * NF), b16),
            pltpu.VMEM((NSRC, 2 * NF), f32),
            dma((5,)),
            dma((rows,)),
            dma((rows,)),
            dma((3, SLOTS, CHUNKS)),
            dma((SLOTS, CHUNKS)),
        ],
        compiler_params=pltpu.CompilerParams(
            collective_id=0, has_side_effects=True, vmem_limit_bytes=50 * 1024 * 1024
        ),
        cost_estimate=pl.CostEstimate(
            flops=12_000_000_000, bytes_accessed=20_000_000, transcendentals=0
        ),
    )(pair_live, strain.T, jnp.asarray(dft_tables()), jnp.asarray(lag_table()), jnp.asarray(band_table()))
    return pl.pallas_call(
        write_out,
        out_shape=jax.ShapeDtypeStruct(shape, b16),
        in_specs=[local] * 3,
        out_specs=anywhere,
        scratch_shapes=[
            pltpu.VMEM((2, NSRC, BLK, NLAG), b16),
            dma((DONE,)),
            dma((2, NSRC)),
        ],
        compiler_params=pltpu.CompilerParams(vmem_limit_bytes=12 * 1024 * 1024),
        cost_estimate=pl.CostEstimate(flops=2_000_000_000, bytes_accessed=8_400_000, transcendentals=0),
    )(*results)


def solution(mesh):
    rows = mesh.shape["row"]
    return jax.shard_map(
        functools.partial(on_device, rows),
        mesh=mesh,
        in_specs=(P(("groups", "row"), None), P(("groups", "row"), None)),
        out_specs=P(("groups", "row"), None, None, None, None),
        check_vma=False,
    )
```
